32 devices in a mesh: dev: 32 (over z, y, x, core).
Axes of the slice: x: 2, y: 2, z: 4, core: 2. Of those that a mesh axis runs over, the one named last changes fastest.
Arguments:
- latents: bfloat16 [256, 256, 384], P('dev'), may hold values from -6 to 6
- cond: bfloat16 [256, 384], P('dev'), may hold values from -6 to 6
- params: bfloat16 [2, 2662400], P(None, 'dev'), may hold values from -2 to 2, as said below
- cotangent: bfloat16 [256, 256, 384], P('dev'), may hold values from -6 to 6
- counts: int32 [32], P('dev'), may hold values from 1 to 8, as said below
Outputs:
- output: bfloat16 [256, 256, 384], P('dev')
- latents_grad: float32 [256, 256, 384], P('dev')
- cond_grad: float32 [256, 384], P('dev')
- param_grads: float32 [2, 2662400], P(None, 'dev')
The draws below stay inside these ranges and needn't reach their ends.
Inputs may be any that keep to these rules, and one draw needn't show every extreme that they name: Each device holds counts of its 8 slots live, the first ones; the rest are padding. Some device is full and some holds one latent. `params`: block i's parameters in the stated order, zeros from 2659584 on.
All inputs are finite; a program needn't handle non-finite values.
Results may differ from the reference program's by a relative error of at most 0.025.
The reference program's roundings to bfloat16 on the way count: a program that leaves them out, or rounds other values in their place, can miss the bound.
Values may be sent and summed in bfloat16 or wider, within the bound.
A program may use at most 192 MiB of HBM per device.

```python
import math
import jax
import jax.numpy as jnp
from jax import lax

D = 384
H = 6
HD = 64
MLP = 1536
SEQ = 256
LAYERS = 2
MAXLAT = 8
LATENTS = 256
PCOUNT = 2659584
PADDED = 2662400


def draw_params(key, part):
    key = jax.random.fold_in(key, 11)
    layout = [(D * 6 * D, D ** (-0.5)), (6 * D, 0.3), (D * 3 * D, D ** (-0.5)), (D, 0.3), (D, 0.3), (D * D, 4.0 * D ** (-0.5)), (D, 0.3), (D * MLP, D ** (-0.5)), (MLP, 0.3), (MLP * D, MLP ** (-0.5)), (D, 0.3)]
    rows_all = []
    for depth in range(LAYERS):
        pieces = []
        for index in range(len(layout)):
            piece_size, spread = layout[index]
            subkey = jax.random.fold_in(jax.random.fold_in(key, depth), index)
            values = jnp.clip(jax.random.normal(subkey, (piece_size,), jnp.float32), -4.0, 4.0) * spread
            pieces.append(jnp.clip(values, -2.0, 2.0))
        pieces.append(jnp.zeros((PADDED - PCOUNT,), jnp.float32))
        rows_all.append(jnp.concatenate(pieces))
    return jnp.stack(rows_all).astype(jnp.bfloat16)


def draw_counts(key, part):
    key = jax.random.fold_in(key, 5)
    device_count = LATENTS // MAXLAT
    key_values, key_first, key_second = jax.random.split(key, 3)
    values = jax.random.randint(key_values, (device_count,), 1, MAXLAT + 1)
    first = jax.random.randint(key_first, (), 0, device_count)
    second = (first + jax.random.randint(key_second, (), 1, device_count)) % device_count
    values = values.at[first].set(MAXLAT)
    values = values.at[second].set(1)
    return values.astype(jnp.int32)


def shard_levels(stream_key, shape, cuts, low, high):
    def one(dim, shards_of):
        steps = jax.random.uniform(jax.random.fold_in(jax.random.fold_in(stream_key, 6), dim), (shards_of,), jnp.float32, low / len(cuts), high / len(cuts))
        return jnp.repeat(jnp.exp(steps), shape[dim] // shards_of).reshape((-1,) + (1,) * (len(shape) - dim - 1))

    level = one(*cuts[0])
    for cut in cuts[1:]:
        level = level * one(*cut)
    return level


def scatter_about(key, extent, scale, reach, cuts=(), held_as=jnp.bfloat16):
    factor_of = shard_levels(key, extent, cuts, -0.22, 0.18) if cuts else 1.0
    values = jax.random.normal(key, extent, jnp.float32) * scale * factor_of
    return jnp.minimum(jnp.maximum(values, -reach), reach).astype(held_as)


def setup_inputs(seed: int = 0) -> dict:
    key_of = jax.random.split(jax.random.key(seed), 6)
    latents = scatter_about(key_of[0], (LATENTS, SEQ, D), 1.0, 6.0, ((0, 32),))
    cond = scatter_about(key_of[1], (LATENTS, D), 1.0, 6.0, ((0, 32),))
    params = draw_params(jax.random.fold_in(key_of[5], 71), 0)
    cotangent = scatter_about(key_of[3], (LATENTS, SEQ, D), 1.0, 6.0, ((0, 32),))
    counts = draw_counts(jax.random.fold_in(key_of[5], 71), 0)
    return {"latents": latents, "cond": cond, "params": params, "cotangent": cotangent, "counts": counts}


epsilon = 1e-06
highest = lax.Precision.HIGHEST

@jax.custom_vjp
def low(v):
    return lax.optimization_barrier(v.astype(jnp.bfloat16)).astype(jnp.float32)

@jax.custom_vjp
def low_back(v):
    return v

def low_keep(v):
    return (low(v), None)

def low_pass(kept, grad):
    return (grad,)

def back_keep(v):
    return (v, None)

def back_low(kept, grad):
    return (low(grad),)
low.defvjp(low_keep, low_pass)
low_back.defvjp(back_keep, back_low)

def piece_layout():
    return [(D, 6 * D), (6 * D,), (D, 3 * D), (D,), (D,), (D, D), (D,), (D, MLP), (MLP,), (MLP, D), (D,)]

def unpack(flat_row):
    pieces = []
    offset = 0
    for shape in piece_layout():
        size_now = math.prod(shape)
        pieces.append(flat_row[offset:offset + size_now].reshape(shape))
        offset += size_now
    return pieces

def normalize(values):
    centered = values - lax.optimization_barrier(jnp.mean(values, axis=-1, keepdims=True))
    variance = lax.optimization_barrier(jnp.mean(centered * centered, axis=-1, keepdims=True))
    return centered * lax.rsqrt(variance + epsilon)

def matmul(left, right):
    return jnp.einsum('...d,de->...e', left, right, precision=highest)

def layer_forward(weights, hidden_in, activ):
    w_ada, b_ada, w_qkv, b_query, b_value, w_out, b_out, w_up, b_up, w_down, b_down = weights
    modulation = low_back(matmul(activ, w_ada) + b_ada)
    shift_a, scale_a, gate_a, shift_b, scale_b, gate_b = [piece[:, None, :] for piece in jnp.split(modulation, 6, axis=-1)]
    normed_a = low(normalize(hidden_in) * (1.0 + scale_a) + shift_a)
    qkv_bias = jnp.concatenate([b_query, jnp.zeros_like(b_query), b_value])
    qkv_all = low(low_back(matmul(normed_a, w_qkv) + qkv_bias))
    latent_count, seq_len = (hidden_in.shape[0], hidden_in.shape[1])
    qkv_all = qkv_all.reshape(latent_count, seq_len, 3, H, HD)
    queries, key_part, value_part = (qkv_all[:, :, 0], qkv_all[:, :, 1], qkv_all[:, :, 2])
    scores = low_back(jnp.einsum('bqhd,bkhd->bhqk', queries, key_part, precision=highest) * HD ** (-0.5))
    soft_weights = jax.nn.softmax(scores, axis=-1)
    context = low(low_back(jnp.einsum('bhqk,bkhd->bqhd', low(soft_weights), value_part, precision=highest)))
    context = context.reshape(latent_count, seq_len, D)
    attended = low_back(matmul(context, w_out) + b_out)
    middle = hidden_in + gate_a * attended
    normed_b = low(normalize(middle) * (1.0 + scale_b) + shift_b)
    pre_act = low_back(matmul(normed_b, w_up) + b_up)
    activated = low(jax.nn.gelu(pre_act, approximate=True))
    branch = low_back(matmul(activated, w_down) + b_down)
    return middle + gate_b * branch

def reference(latents, cond, params, cotangent, counts):
    group_size = 16
    groups = LATENTS // group_size
    live_mask = (jnp.arange(MAXLAT)[None, :] < counts[:, None]).reshape(-1).astype(jnp.float32)
    weights_all = params.astype(jnp.float32)[:, :PCOUNT]
    hidden = latents.astype(jnp.float32)
    cond_float = cond.astype(jnp.float32)
    cot_float = cotangent.astype(jnp.float32) * live_mask[:, None, None]

    def run(weights_now, hidden_now, cond_part):
        activ = low(jax.nn.silu(cond_part))
        for depth in range(LAYERS):
            hidden_now = layer_forward(unpack(weights_now[depth]), hidden_now, activ)
        return hidden_now

    def group_step(totals, block_item):
        hidden_part, cond_part, cot_part = block_item
        result, pullback = jax.vjp(run, weights_all, hidden_part, cond_part)
        grad_weights, grad_hidden, grad_cond = pullback(cot_part)
        return (totals + grad_weights, (result, grad_hidden, grad_cond))

    def grouped(values):
        return values.reshape((groups, group_size) + values.shape[1:])
    totals, (outputs, grad_latents, grad_cond) = lax.scan(group_step, jnp.zeros((LAYERS, PCOUNT), jnp.float32), (grouped(hidden), grouped(cond_float), grouped(cot_float)))
    output = (outputs.reshape(LATENTS, SEQ, D) * live_mask[:, None, None]).astype(jnp.bfloat16)
    param_grads = jnp.pad(totals, ((0, 0), (0, PADDED - PCOUNT)))
    return (output, grad_latents.reshape(LATENTS, SEQ, D), grad_cond.reshape(LATENTS, D), param_grads)
```

```python
import functools

import jax
import jax.numpy as jnp
from jax import lax
from jax.experimental import pallas as pl
from jax.experimental.pallas import tpu as pltpu
from jax.sharding import PartitionSpec as P

D = 384
H = 6
HD = 64
MLP = 1536
SEQ = 256
LAYERS = 2
PAIR = 2
ROWS = PAIR * SEQ
LANES = 128
EPS = 1e-06
GELU_A = 0.7978845608028654
GELU_B = 0.044715
F32 = jnp.float32
BF16 = jnp.bfloat16

R_ADA = 0
R_BADA = 6912
R_QKV = 6930
R_BQ = 10386
R_BV = 10389
R_O = 10392
R_BO = 11544
R_1 = 11547
R_B1 = 16155
R_2 = 16167
R_B2 = 20775
R_END = 20778

VMEM_LIMIT = 62 * 1024 * 1024


def mm(a, b):
    return lax.dot_general(a, b, (((1,), (0,)), ((), ())), preferred_element_type=F32)


def mm_bt(a, b):
    return lax.dot_general(a, b, (((1,), (1,)), ((), ())), preferred_element_type=F32)


def mm_at(a, b):
    return lax.dot_general(a, b, (((0,), (0,)), ((), ())), preferred_element_type=F32)


def slot_of(order, j):
    return sum(((j >> bit) & 1) << place for place, bit in enumerate(order))


def normalize(values):
    centered = values - jnp.mean(values, axis=-1, keepdims=True)
    inv_std = lax.rsqrt(jnp.mean(centered * centered, axis=-1, keepdims=True) + EPS)
    return centered * inv_std, inv_std


def norm_back(grad, normed, inv_std):
    mean_grad = jnp.mean(grad, axis=-1, keepdims=True)
    mean_cross = jnp.mean(grad * normed, axis=-1, keepdims=True)
    return inv_std * (grad - mean_grad - normed * mean_cross)


def per_latent(values):
    return values.reshape(PAIR, SEQ, values.shape[-1])


def flat_rows(values):
    return values.reshape(ROWS, values.shape[-1])


def load_weights(order, chunk, me, half_a, half_b, activ, stage, flat, sem, w):
    n = stage.shape[0]
    first = pltpu.make_async_copy(half_a, stage.at[pl.ds(0, n // 2)], sem.at[0])
    second = pltpu.make_async_copy(half_b, stage.at[pl.ds(n // 2, n // 2)], sem.at[1])
    first.start()
    second.start()
    first.wait()
    second.wait()
    padded = stage.shape[1]

    def spread(owner, carry):
        slot = slot_of(order, owner ^ me)
        flat[pl.ds(owner * chunk, padded), :] = stage[slot].astype(F32)
        return carry

    lax.fori_loop(0, n, spread, 0)

    def matrix(ref, row, depth, width):
        count = width // LANES
        for c in range(count):
            ref[:, c * LANES : (c + 1) * LANES] = flat[
                pl.ds(row + c, depth, stride=count), :
            ].astype(BF16)

    def vector(ref, row, width, start=0):
        for c in range(width // LANES):
            ref[:, start + c * LANES : start + (c + 1) * LANES] = flat[row + c : row + c + 1, :]

    matrix(w["ada"], R_ADA, D, 6 * D)
    matrix(w["qkv"], R_QKV, D, 3 * D)
    matrix(w["o"], R_O, D, D)
    matrix(w["1"], R_1, D, MLP)
    matrix(w["2"], R_2, MLP, D)
    vector(w["bada"], R_BADA, 6 * D)
    w["bqkv"][...] = jnp.zeros((1, 3 * D), F32)
    vector(w["bqkv"], R_BQ, D)
    vector(w["bqkv"], R_BV, D, 2 * D)
    vector(w["bo"], R_BO, D)
    vector(w["b1"], R_B1, MLP)
    vector(w["b2"], R_B2, D)
    modul = mm(activ[...], w["ada"][...]) + w["bada"][...]
    for latent in range(16):
        w["mods"][latent] = modul[latent : latent + 1, :]


WEIGHT_SCRATCH = {
    "ada": ((D, 6 * D), BF16),
    "qkv": ((D, 3 * D), BF16),
    "o": ((D, D), BF16),
    "1": ((D, MLP), BF16),
    "2": ((MLP, D), BF16),
    "bada": ((1, 6 * D), F32),
    "bqkv": ((1, 3 * D), F32),
    "bo": ((1, D), F32),
    "b1": ((1, MLP), F32),
    "b2": ((1, D), F32),
    "mods": ((16, 1, 6 * D), F32),
}
ACT_SCRATCH = {
    "n1": ((ROWS, D), BF16),
    "qkvv": ((ROWS, 3 * D), BF16),
    "ctx": ((ROWS, D), BF16),
    "n2": ((ROWS, D), BF16),
    "act": ((ROWS, MLP), BF16),
    "branch": ((ROWS, D), F32),
}
BACK_SCRATCH = {
    "probs": ((PAIR * H, SEQ, SEQ), BF16),
    "slope": ((ROWS, MLP), BF16),
    "dpre": ((ROWS, MLP), BF16),
    "dbranch": ((ROWS, D), BF16),
    "dctx": ((ROWS, D), BF16),
    "dqkv": ((ROWS, 3 * D), BF16),
    "gqkv": ((D, 3 * D), F32),
    "go": ((D, D), F32),
    "g1": ((D, MLP), F32),
    "g2": ((MLP, D), F32),
    "gbqkv": ((1, 3 * D), F32),
    "gbo": ((1, D), F32),
    "gb1": ((1, MLP), F32),
    "gb2": ((1, D), F32),
    "dmods": ((16, 1, 6 * D), F32),
}


def head_masks():
    lane = lax.broadcasted_iota(jnp.int32, (SEQ, LANES), 1)
    return lane < HD


def split_heads(values, low_half):
    zero = jnp.zeros_like(values)
    return jnp.where(low_half, values, zero), jnp.where(low_half, zero, values)


def forward(step, x, w, s, keep):
    mods = w["mods"][pl.ds(step * PAIR, PAIR)]
    shift_a, scale_a, gate_a, shift_b, scale_b, gate_b = [
        mods[:, :, p * D : (p + 1) * D] for p in range(6)
    ]
    normed_x, inv_a = normalize(x)
    s["n1"][...] = flat_rows(per_latent(normed_x) * (1.0 + scale_a) + shift_a).astype(BF16)
    s["qkvv"][...] = (mm(s["n1"][...], w["qkv"][...]) + w["bqkv"][...]).astype(BF16)

    def attend(index, carry):
        latent = index // (H // 2)
        pair = index % (H // 2)
        rows = pl.ds(pl.multiple_of(latent * SEQ, SEQ), SEQ)
        low_half = head_masks()

        def lanes(part):
            return pl.ds(pl.multiple_of(part * D + pair * LANES, LANES), LANES)

        q_heads = split_heads(s["qkvv"][rows, lanes(0)] * BF16(HD**-0.5), low_half)
        keys = s["qkvv"][rows, lanes(1)]
        v_heads = split_heads(s["qkvv"][rows, lanes(2)], low_half)
        both = []
        for head in range(2):
            scores = mm_bt(q_heads[head], keys)
            top = jnp.max(scores, axis=-1, keepdims=True)
            raised = jnp.exp(scores - top)
            probs = raised * (1.0 / jnp.sum(raised, axis=-1, keepdims=True))
            probs = probs.astype(BF16)
            if keep:
                s["probs"][index * 2 + head] = probs
            both.append(probs)
        context = mm(jnp.concatenate(both, axis=1), jnp.concatenate(v_heads, axis=0))
        s["ctx"][rows, lanes(0)] = context.astype(BF16)
        return carry

    lax.fori_loop(0, PAIR * H // 2, attend, 0)
    attended = mm(s["ctx"][...], w["o"][...]) + w["bo"][...]
    middle = x + flat_rows(gate_a * per_latent(attended))
    normed_mid, inv_b = normalize(middle)
    s["n2"][...] = flat_rows(per_latent(normed_mid) * (1.0 + scale_b) + shift_b).astype(BF16)

    def hidden(index, carry):
        cols = pl.ds(pl.multiple_of(index * D, D), D)
        pre = mm(s["n2"][...], w["1"][:, cols]) + w["b1"][:, cols]
        square = pre * pre
        tanh = jnp.tanh(pre * (GELU_A + GELU_A * GELU_B * square))
        half = 0.5 * (1.0 + tanh)
        s["act"][:, cols] = (pre * half).astype(BF16)
        if keep:
            inner = GELU_A + 3.0 * GELU_A * GELU_B * square
            slope = half + 0.5 * pre * (1.0 - tanh * tanh) * inner
            s["slope"][:, cols] = slope.astype(BF16)
        return carry

    lax.fori_loop(0, MLP // D, hidden, 0)
    branch = mm(s["act"][...], w["2"][...]) + w["b2"][...]
    result = middle + flat_rows(gate_b * per_latent(branch))
    return result, branch, attended, normed_x, inv_a, normed_mid, inv_b, mods


def forward_kernel(order, chunk, names, scalars, half_a, half_b, activ, x_ref, y_ref, stage, flat, sem, *scratch):
    refs = dict(zip(names, scratch))
    step = pl.program_id(0)
    count, me = scalars[0], scalars[1]

    @pl.when(step == 0)
    def _():
        load_weights(order, chunk, me, half_a, half_b, activ, stage, flat, sem, refs)

    @pl.when(step * PAIR < count)
    def _():
        x = flat_rows(x_ref[...].astype(F32))
        y_ref[...] = per_latent(forward(step, x, refs, refs, False)[0])

    @pl.when(step * PAIR >= count)
    def _():
        y_ref[...] = jnp.zeros_like(y_ref)


def backward_step(step, x, grad, w, s, branch, attended, normed_x, inv_a, normed_mid, inv_b, mods):
    shift_a, scale_a, gate_a, shift_b, scale_b, gate_b = [
        mods[:, :, p * D : (p + 1) * D] for p in range(6)
    ]

    def put_mod(piece, values):
        s["dmods"][pl.ds(step * PAIR, PAIR), :, piece * D : (piece + 1) * D] = jnp.sum(
            per_latent(values), axis=1, keepdims=True
        )

    put_mod(5, grad * branch)
    dbranch = flat_rows(gate_b * per_latent(grad)).astype(BF16)
    s["dbranch"][...] = dbranch
    s["gb2"][...] += jnp.sum(dbranch.astype(F32), axis=0, keepdims=True)

    def hidden(index, carry):
        cols = pl.ds(pl.multiple_of(index * D, D), D)
        s["g2"][cols, :] += mm_at(s["act"][:, cols], s["dbranch"][...])
        dact = mm_bt(s["dbranch"][...], w["2"][cols, :])
        dpre = (dact * s["slope"][:, cols].astype(F32)).astype(BF16)
        s["dpre"][:, cols] = dpre
        s["gb1"][:, cols] += jnp.sum(dpre.astype(F32), axis=0, keepdims=True)
        s["g1"][:, cols] += mm_at(s["n2"][...], dpre)
        return carry

    lax.fori_loop(0, MLP // D, hidden, 0)
    dnorm_b = mm_bt(s["dpre"][...], w["1"][...])
    put_mod(4, dnorm_b * normed_mid)
    put_mod(3, dnorm_b)
    grad_mid = grad + norm_back(
        flat_rows(per_latent(dnorm_b) * (1.0 + scale_b)), normed_mid, inv_b
    )
    put_mod(2, grad_mid * attended)
    dattended = flat_rows(gate_a * per_latent(grad_mid)).astype(BF16)
    s["gbo"][...] += jnp.sum(dattended.astype(F32), axis=0, keepdims=True)
    s["go"][...] += mm_at(s["ctx"][...], dattended)
    s["dctx"][...] = mm_bt(dattended, w["o"][...]).astype(BF16)

    def attend(index, carry):
        latent = index // (H // 2)
        pair = index % (H // 2)
        rows = pl.ds(pl.multiple_of(latent * SEQ, SEQ), SEQ)
        low_half = head_masks()

        def lanes(part):
            return pl.ds(pl.multiple_of(part * D + pair * LANES, LANES), LANES)

        q_heads = split_heads(s["qkvv"][rows, lanes(0)] * BF16(HD**-0.5), low_half)
        k_heads = split_heads(s["qkvv"][rows, lanes(1)] * BF16(HD**-0.5), low_half)
        values = s["qkvv"][rows, lanes(2)]
        dctx = s["dctx"][rows, lanes(0)]
        dctx_heads = split_heads(dctx, low_half)
        cross = dctx.astype(F32) * s["ctx"][rows, lanes(0)].astype(F32)
        dscores = []
        for head in range(2):
            own = jnp.where(low_half == (head == 0), cross, 0.0)
            row_dot = jnp.sum(own, axis=-1, keepdims=True)
            dprobs = mm_bt(dctx_heads[head], values)
            probs = s["probs"][index * 2 + head].astype(F32)
            dscores.append((probs * (dprobs - row_dot)).astype(BF16))
        dquery = mm(jnp.concatenate(dscores, axis=1), jnp.concatenate(k_heads, axis=0))
        dkey = mm_at(dscores[0], q_heads[0]) + mm_at(dscores[1], q_heads[1])
        dvalue = mm_at(s["probs"][index * 2], dctx_heads[0]) + mm_at(
            s["probs"][index * 2 + 1], dctx_heads[1]
        )
        s["dqkv"][rows, lanes(0)] = dquery.astype(BF16)
        s["dqkv"][rows, lanes(1)] = dkey.astype(BF16)
        s["dqkv"][rows, lanes(2)] = dvalue.astype(BF16)
        return carry

    lax.fori_loop(0, PAIR * H // 2, attend, 0)
    dqkv = s["dqkv"][...]
    s["gqkv"][...] += mm_at(s["n1"][...], dqkv)
    s["gbqkv"][...] += jnp.sum(dqkv.astype(F32), axis=0, keepdims=True)
    dnorm_a = mm_bt(dqkv, w["qkv"][...])
    put_mod(1, dnorm_a * normed_x)
    put_mod(0, dnorm_a)
    return grad_mid + norm_back(
        flat_rows(per_latent(dnorm_a) * (1.0 + scale_a)), normed_x, inv_a
    )


def pack_grads(order, chunk, me, activ, stage, flat, sem, w, s, out_grads, dactiv_ref):
    n, padded = stage.shape[0], stage.shape[1]

    def matrix(values_of, row, depth, width):
        count = width // LANES
        for c in range(count):
            flat[pl.ds(row + c, depth, stride=count), :] = values_of(c)

    def of_ref(ref):
        return lambda c: ref[:, c * LANES : (c + 1) * LANES]

    def vector(value, row, width, start=0):
        for c in range(width // LANES):
            flat[row + c : row + c + 1, :] = value[:, start + c * LANES : start + (c + 1) * LANES]

    dmods = jnp.concatenate([s["dmods"][latent] for latent in range(16)], axis=0).astype(BF16)
    dmods_wide = dmods.astype(F32)
    dactiv_ref[...] = mm_bt(dmods, w["ada"][...])
    left = activ[...]
    matrix(lambda c: mm_at(left, dmods[:, c * LANES : (c + 1) * LANES]), R_ADA, D, 6 * D)
    vector(jnp.sum(dmods_wide, axis=0, keepdims=True), R_BADA, 6 * D)
    matrix(of_ref(s["gqkv"]), R_QKV, D, 3 * D)
    vector(s["gbqkv"], R_BQ, D)
    vector(s["gbqkv"], R_BV, D, 2 * D)
    matrix(of_ref(s["go"]), R_O, D, D)
    vector(s["gbo"], R_BO, D)
    matrix(of_ref(s["g1"]), R_1, D, MLP)
    vector(s["gb1"], R_B1, MLP)
    matrix(of_ref(s["g2"]), R_2, MLP, D)
    vector(s["gb2"], R_B2, D)
    flat[R_END : flat.shape[0], :] = jnp.zeros((flat.shape[0] - R_END, LANES), F32)

    def gather(owner, carry):
        slot = slot_of(order, owner ^ me)
        stage[slot] = flat[pl.ds(owner * chunk, padded), :].astype(BF16)
        return carry

    lax.fori_loop(0, n, gather, 0)
    copy = pltpu.make_async_copy(stage, out_grads, sem.at[0])
    copy.start()
    copy.wait()


def backward_kernel(order, chunk, names, last, scalars, half_a, half_b, activ, x_ref, g_ref, *rest):
    if last:
        out_ref, *rest = rest
    gin_ref, dactiv_ref, out_grads, stage, flat, sem, *scratch = rest
    refs = dict(zip(names, scratch))
    step = pl.program_id(0)
    count, me = scalars[0], scalars[1]

    @pl.when(step == 0)
    def _():
        load_weights(order, chunk, me, half_a, half_b, activ, stage, flat, sem, refs)
        for name in ("gqkv", "go", "g1", "g2", "gbqkv", "gbo", "gb1", "gb2", "dmods"):
            refs[name][...] = jnp.zeros_like(refs[name])

    @pl.when(step * PAIR < count)
    def _():
        x = flat_rows(x_ref[...].astype(F32))
        result, branch, *kept = forward(step, x, refs, refs, True)
        grad = g_ref[...].astype(F32)
        if last:
            latent = lax.broadcasted_iota(jnp.int32, (PAIR, SEQ, D), 0) + step * PAIR
            live = latent < count
            out_ref[...] = jnp.where(live, per_latent(result), 0.0).astype(BF16)
            grad = jnp.where(live, grad, 0.0)
        gin_ref[...] = per_latent(
            backward_step(step, x, flat_rows(grad), refs, refs, branch, *kept)
        )

    @pl.when(step * PAIR >= count)
    def _():
        gin_ref[...] = jnp.zeros_like(gin_ref)
        if last:
            out_ref[...] = jnp.zeros_like(out_ref)

    @pl.when(step == pl.num_programs(0) - 1)
    def _():
        pack_grads(order, chunk, me, activ, stage, flat, sem, refs, refs, out_grads, dactiv_ref)


def scratch_of(parts):
    names, shapes = [], []
    for part in parts:
        for name, (shape, dtype) in part.items():
            names.append(name)
            shapes.append(pltpu.VMEM(shape, dtype))
    return tuple(names), shapes


def run_forward(order, chunk, scalars, halves, activ, x):
    n, padded = 2 * halves[0].shape[0], halves[0].shape[1]
    names, shapes = scratch_of([WEIGHT_SCRATCH, ACT_SCRATCH])
    block = pl.BlockSpec((PAIR, SEQ, D), lambda i, sc: (i, 0, 0))
    whole = pl.BlockSpec((16, D), lambda i, sc: (0, 0))
    hbm = pl.BlockSpec(memory_space=pl.ANY)
    return pl.pallas_call(
        functools.partial(forward_kernel, order, chunk, names),
        grid_spec=pltpu.PrefetchScalarGridSpec(
            num_scalar_prefetch=1,
            grid=(x.shape[0] // PAIR,),
            in_specs=[hbm, hbm, whole, block],
            out_specs=block,
            scratch_shapes=[
                pltpu.VMEM((n, padded, LANES), BF16),
                pltpu.VMEM(((n - 1) * chunk + padded, LANES), F32),
                pltpu.SemaphoreType.DMA((2,)),
            ]
            + shapes,
        ),
        out_shape=jax.ShapeDtypeStruct(x.shape, F32),
        compiler_params=pltpu.CompilerParams(vmem_limit_bytes=VMEM_LIMIT),
        cost_estimate=pl.CostEstimate(
            flops=8_000_000_000, bytes_accessed=20_000_000, transcendentals=6_000_000
        ),
        name="block_forward",
    )(scalars, *halves, activ, x)


def run_backward(order, chunk, scalars, halves, activ, x, grad, last):
    n, padded = 2 * halves[0].shape[0], halves[0].shape[1]
    names, shapes = scratch_of([WEIGHT_SCRATCH, ACT_SCRATCH, BACK_SCRATCH])
    block = pl.BlockSpec((PAIR, SEQ, D), lambda i, sc: (i, 0, 0))
    whole = pl.BlockSpec((16, D), lambda i, sc: (0, 0))
    hbm = pl.BlockSpec(memory_space=pl.ANY)
    outs = [
        jax.ShapeDtypeStruct(x.shape, F32),
        jax.ShapeDtypeStruct((16, D), F32),
        jax.ShapeDtypeStruct((n, padded, LANES), BF16),
    ]
    out_specs = [block, whole, hbm]
    if last:
        outs = [jax.ShapeDtypeStruct(x.shape, BF16)] + outs
        out_specs = [block] + out_specs
    return pl.pallas_call(
        functools.partial(backward_kernel, order, chunk, names, last),
        grid_spec=pltpu.PrefetchScalarGridSpec(
            num_scalar_prefetch=1,
            grid=(x.shape[0] // PAIR,),
            in_specs=[hbm, hbm, whole, block, block],
            out_specs=out_specs,
            scratch_shapes=[
                pltpu.VMEM((n, padded, LANES), BF16),
                pltpu.VMEM(((n - 1) * chunk + padded, LANES), F32),
                pltpu.SemaphoreType.DMA((2,)),
            ]
            + shapes,
        ),
        out_shape=outs,
        compiler_params=pltpu.CompilerParams(vmem_limit_bytes=VMEM_LIMIT),
        cost_estimate=pl.CostEstimate(
            flops=32_000_000_000, bytes_accessed=40_000_000, transcendentals=6_000_000
        ),
        name="block_backward",
    )(scalars, *halves, activ, x, grad)


def swap(values, bit, n):
    return lax.ppermute(values, "dev", [(i, i ^ (1 << bit)) for i in range(n)])


def gather_halves(order, n, shard):
    held = shard
    for bit in order[:-1]:
        held = jnp.concatenate([held, swap(held, bit, n)], axis=0)
    return held, swap(held, order[-1], n)


def scatter_sum(order, n, parts):
    for bit in order[::-1]:
        half = parts.shape[0] // 2
        sent = swap(parts[half:], bit, n)
        total = parts[:half].astype(F32) + sent.astype(F32)
        parts = total.astype(BF16) if half > 1 else total
    return parts


def shards(latents, cond, params, cotangent, counts):
    n = lax.axis_size("dev")
    chunk = params.shape[1] // LANES
    padded = (chunk + 15) // 16 * 16
    bits = n.bit_length() - 1
    first = list(range(bits - 1, -1, -1))
    second = list(first)
    if bits > 2:
        second[-2], second[-3] = second[-3], second[-2]
    orders = [tuple(first), tuple(second)]
    scalars = jnp.stack([counts[0], lax.axis_index("dev").astype(jnp.int32)])
    cond_float = cond.astype(F32)
    activ = jax.nn.silu(cond_float).astype(BF16)
    activ = jnp.pad(activ, ((0, 16 - activ.shape[0]), (0, 0)))
    rows = params.reshape(LAYERS, chunk, LANES)
    rows = jnp.pad(rows, ((0, 0), (0, padded - chunk), (0, 0)))
    weights = [gather_halves(orders[i], n, rows[i : i + 1]) for i in range(LAYERS)]
    middle = run_forward(orders[0], chunk, scalars, weights[0], activ, latents)
    output, grad_mid, dactiv_2, parts_2 = run_backward(
        orders[1], chunk, scalars, weights[1], activ, middle, cotangent, True
    )
    sum_2 = scatter_sum(orders[1], n, parts_2)
    grad_in, dactiv_1, parts_1 = run_backward(
        orders[0], chunk, scalars, weights[0], activ, latents, grad_mid, False
    )
    sum_1 = scatter_sum(orders[0], n, parts_1)
    param_grads = jnp.concatenate([sum_1, sum_2], axis=0)[:, :chunk].reshape(LAYERS, chunk * LANES)
    _, silu_pull = jax.vjp(jax.nn.silu, cond_float)
    cond_grad = silu_pull((dactiv_1 + dactiv_2)[: cond.shape[0]])[0]
    return (output, grad_in, cond_grad, param_grads)


def solution(mesh):
    return jax.shard_map(
        shards,
        mesh=mesh,
        in_specs=(
            P("dev", None, None),
            P("dev", None),
            P(None, "dev"),
            P("dev", None, None),
            P("dev"),
        ),
        out_specs=(P("dev", None, None), P("dev", None, None), P("dev", None), P(None, "dev")),
        check_vma=False,
    )
```

```python
import functools

import jax
import jax.numpy as jnp
from jax import lax
from jax.experimental import pallas as pl
from jax.experimental.pallas import tpu as pltpu
from jax.sharding import PartitionSpec as P

D = 384
H = 6
HD = 64
MLP = 1536
SEQ = 256
LAYERS = 2
PAIR = 2
ROWS = PAIR * SEQ
LANES = 128
EPS = 1e-06
GELU_A = 0.7978845608028654
GELU_B = 0.044715
F32 = jnp.float32
BF16 = jnp.bfloat16

R_ADA = 0
R_BADA = 6912
R_QKV = 6930
R_BQ = 10386
R_BV = 10389
R_O = 10392
R_BO = 11544
R_1 = 11547
R_B1 = 16155
R_2 = 16167
R_B2 = 20775
R_END = 20778

VMEM_LIMIT = 62 * 1024 * 1024


def mm(a, b):
    return lax.dot_general(a, b, (((1,), (0,)), ((), ())), preferred_element_type=F32)


def mm_bt(a, b):
    return lax.dot_general(a, b, (((1,), (1,)), ((), ())), preferred_element_type=F32)


def mm_at(a, b):
    return lax.dot_general(a, b, (((0,), (0,)), ((), ())), preferred_element_type=F32)


def slot_of(order, owner, me):
    if order is None:
        return owner
    j = owner ^ me
    return sum(((j >> bit) & 1) << place for place, bit in enumerate(order))


def normalize(values):
    centered = values - jnp.mean(values, axis=-1, keepdims=True)
    inv_std = lax.rsqrt(jnp.mean(centered * centered, axis=-1, keepdims=True) + EPS)
    return centered * inv_std, inv_std


def norm_back(grad, normed, inv_std):
    mean_grad = jnp.mean(grad, axis=-1, keepdims=True)
    mean_cross = jnp.mean(grad * normed, axis=-1, keepdims=True)
    return inv_std * (grad - mean_grad - normed * mean_cross)


def per_latent(values):
    return values.reshape(PAIR, SEQ, values.shape[-1])


def flat_rows(values):
    return values.reshape(ROWS, values.shape[-1])


def load_weights(order, chunk, me, half_a, half_b, activ, stage, flat, sem, w):
    n = stage.shape[0]
    held = n // 2
    source = half_b.at[pl.ds(half_b.shape[0] - held, held)]
    first = pltpu.make_async_copy(half_a.at[pl.ds(0, held)], stage.at[pl.ds(0, held)], sem.at[0])
    second = pltpu.make_async_copy(source, stage.at[pl.ds(held, held)], sem.at[1])
    first.start()
    second.start()
    first.wait()
    second.wait()
    padded = stage.shape[1]

    def spread(owner, carry):
        slot = slot_of(order[0], owner, me)
        flat[pl.ds(owner * chunk, padded), :] = stage[slot].astype(F32)
        return carry

    lax.fori_loop(0, n, spread, 0)

    def matrix(ref, row, depth, width):
        count = width // LANES
        for c in range(count):
            ref[:, c * LANES : (c + 1) * LANES] = flat[
                pl.ds(row + c, depth, stride=count), :
            ].astype(BF16)

    def vector(ref, row, width, start=0):
        for c in range(width // LANES):
            ref[:, start + c * LANES : start + (c + 1) * LANES] = flat[row + c : row + c + 1, :]

    matrix(w["ada"], R_ADA, D, 6 * D)
    matrix(w["qkv"], R_QKV, D, 3 * D)
    matrix(w["o"], R_O, D, D)
    matrix(w["1"], R_1, D, MLP)
    matrix(w["2"], R_2, MLP, D)
    vector(w["bada"], R_BADA, 6 * D)
    w["bqkv"][...] = jnp.zeros((1, 3 * D), F32)
    vector(w["bqkv"], R_BQ, D)
    vector(w["bqkv"], R_BV, D, 2 * D)
    vector(w["bo"], R_BO, D)
    vector(w["b1"], R_B1, MLP)
    vector(w["b2"], R_B2, D)
    modul = mm(activ[...], w["ada"][...]) + w["bada"][...]
    for latent in range(16):
        w["mods"][latent] = modul[latent : latent + 1, :]


WEIGHT_SCRATCH = {
    "ada": ((D, 6 * D), BF16),
    "qkv": ((D, 3 * D), BF16),
    "o": ((D, D), BF16),
    "1": ((D, MLP), BF16),
    "2": ((MLP, D), BF16),
    "bada": ((1, 6 * D), F32),
    "bqkv": ((1, 3 * D), F32),
    "bo": ((1, D), F32),
    "b1": ((1, MLP), F32),
    "b2": ((1, D), F32),
    "mods": ((16, 1, 6 * D), F32),
}
ACT_SCRATCH = {
    "n1": ((ROWS, D), BF16),
    "qkvv": ((ROWS, 3 * D), BF16),
    "ctx": ((ROWS, D), BF16),
    "n2": ((ROWS, D), BF16),
    "act": ((ROWS, MLP), BF16),
    "branch": ((ROWS, D), F32),
}
BACK_SCRATCH = {
    "probs": ((PAIR * H, SEQ, SEQ), BF16),
    "slope": ((ROWS, MLP), BF16),
    "dpre": ((ROWS, MLP), BF16),
    "dbranch": ((ROWS, D), BF16),
    "dbrancht": ((D, ROWS), BF16),
    "n2t": ((D, ROWS), BF16),
    "dctx": ((ROWS, D), BF16),
    "dqkv": ((ROWS, 3 * D), BF16),
    "gqkv": ((D, 3 * D), F32),
    "go": ((D, D), F32),
    "g1": ((D, MLP), F32),
    "g2": ((D, MLP), F32),
    "gbqkv": ((1, 3 * D), F32),
    "gbo": ((1, D), F32),
    "gb1": ((1, MLP), F32),
    "gb2": ((1, D), F32),
    "dmods": ((16, 1, 6 * D), F32),
}


def head_masks():
    lane = lax.broadcasted_iota(jnp.int32, (SEQ, LANES), 1)
    return lane < HD


def split_heads(values, low_half):
    zero = jnp.zeros_like(values)
    return jnp.where(low_half, values, zero), jnp.where(low_half, zero, values)


def forward(step, x, w, s, keep):
    mods = w["mods"][pl.ds(step * PAIR, PAIR)]
    shift_a, scale_a, gate_a, shift_b, scale_b, gate_b = [
        mods[:, :, p * D : (p + 1) * D] for p in range(6)
    ]
    normed_x, inv_a = normalize(x)
    s["n1"][...] = flat_rows(per_latent(normed_x) * (1.0 + scale_a) + shift_a).astype(BF16)
    s["qkvv"][...] = (mm(s["n1"][...], w["qkv"][...]) + w["bqkv"][...]).astype(BF16)

    def attend(index):
        latent = index // (H // 2)
        pair = index % (H // 2)
        rows = pl.ds(latent * SEQ, SEQ)
        low_half = head_masks()

        def lanes(part):
            return pl.ds(part * D + pair * LANES, LANES)

        q_heads = split_heads(s["qkvv"][rows, lanes(0)] * BF16(HD**-0.5), low_half)
        keys = s["qkvv"][rows, lanes(1)]
        v_heads = split_heads(s["qkvv"][rows, lanes(2)], low_half)
        both = []
        for head in range(2):
            scores = mm_bt(q_heads[head], keys)
            top = jnp.max(scores, axis=-1, keepdims=True)
            raised = jnp.exp(scores - top)
            probs = raised * (1.0 / jnp.sum(raised, axis=-1, keepdims=True))
            probs = probs.astype(BF16)
            if keep:
                s["probs"][index * 2 + head] = probs
            both.append(probs)
        context = mm(jnp.concatenate(both, axis=1), jnp.concatenate(v_heads, axis=0))
        s["ctx"][rows, lanes(0)] = context.astype(BF16)

    for index in range(PAIR * H // 2):
        attend(index)
    attended = mm(s["ctx"][...], w["o"][...]) + w["bo"][...]
    middle = x + flat_rows(gate_a * per_latent(attended))
    normed_mid, inv_b = normalize(middle)
    s["n2"][...] = flat_rows(per_latent(normed_mid) * (1.0 + scale_b) + shift_b).astype(BF16)

    def hidden(index):
        cols = pl.ds(index * D, D)
        pre = mm(s["n2"][...], w["1"][:, cols]) + w["b1"][:, cols]
        square = pre * pre
        tanh = jnp.tanh(pre * (GELU_A + GELU_A * GELU_B * square))
        half = 0.5 * (1.0 + tanh)
        s["act"][:, cols] = (pre * half).astype(BF16)
        if keep:
            inner = GELU_A + 3.0 * GELU_A * GELU_B * square
            slope = half + 0.5 * pre * (1.0 - tanh * tanh) * inner
            s["slope"][:, cols] = slope.astype(BF16)

    for index in range(MLP // D):
        hidden(index)
    branch = mm(s["act"][...], w["2"][...]) + w["b2"][...]
    result = middle + flat_rows(gate_b * per_latent(branch))
    return result, branch, attended, normed_x, inv_a, normed_mid, inv_b, mods


def forward_kernel(order, chunk, names, scalars, half_a, half_b, activ, x_ref, y_ref, stage, flat, sem, *scratch):
    refs = dict(zip(names, scratch))
    step = pl.program_id(0)
    count, me = scalars[0], scalars[1]

    @pl.when(step == 0)
    def _():
        load_weights(order, chunk, me, half_a, half_b, activ, stage, flat, sem, refs)

    @pl.when(step * PAIR < count)
    def _():
        x = flat_rows(x_ref[...].astype(F32))
        y_ref[...] = per_latent(forward(step, x, refs, refs, False)[0])

    @pl.when(step * PAIR >= count)
    def _():
        y_ref[...] = jnp.zeros_like(y_ref)


def backward_step(step, x, grad, w, s, branch, attended, normed_x, inv_a, normed_mid, inv_b, mods):
    shift_a, scale_a, gate_a, shift_b, scale_b, gate_b = [
        mods[:, :, p * D : (p + 1) * D] for p in range(6)
    ]

    def put_mod(piece, values):
        s["dmods"][pl.ds(step * PAIR, PAIR), :, piece * D : (piece + 1) * D] = jnp.sum(
            per_latent(values), axis=1, keepdims=True
        )

    put_mod(5, grad * branch)
    dbranch = flat_rows(gate_b * per_latent(grad)).astype(BF16)
    s["dbranch"][...] = dbranch
    s["dbrancht"][...] = dbranch.T
    s["n2t"][...] = s["n2"][...].T
    s["gb2"][...] += jnp.sum(dbranch.astype(F32), axis=0, keepdims=True)

    def hidden(index):
        cols = pl.ds(index * D, D)
        s["g2"][:, cols] += mm(s["dbrancht"][...], s["act"][:, cols])
        dact = mm_bt(s["dbranch"][...], w["2"][cols, :])
        dpre = (dact * s["slope"][:, cols].astype(F32)).astype(BF16)
        s["dpre"][:, cols] = dpre
        s["gb1"][:, cols] += jnp.sum(dpre.astype(F32), axis=0, keepdims=True)
        s["g1"][:, cols] += mm(s["n2t"][...], dpre)

    for index in range(MLP // D):
        hidden(index)
    dnorm_b = mm_bt(s["dpre"][...], w["1"][...])
    put_mod(4, dnorm_b * normed_mid)
    put_mod(3, dnorm_b)
    grad_mid = grad + norm_back(
        flat_rows(per_latent(dnorm_b) * (1.0 + scale_b)), normed_mid, inv_b
    )
    put_mod(2, grad_mid * attended)
    dattended = flat_rows(gate_a * per_latent(grad_mid)).astype(BF16)
    s["gbo"][...] += jnp.sum(dattended.astype(F32), axis=0, keepdims=True)
    s["go"][...] += mm_at(s["ctx"][...], dattended)
    s["dctx"][...] = mm_bt(dattended, w["o"][...]).astype(BF16)

    def attend(index):
        latent = index // (H // 2)
        pair = index % (H // 2)
        rows = pl.ds(latent * SEQ, SEQ)
        low_half = head_masks()

        def lanes(part):
            return pl.ds(part * D + pair * LANES, LANES)

        q_heads = split_heads(s["qkvv"][rows, lanes(0)] * BF16(HD**-0.5), low_half)
        k_heads = split_heads(s["qkvv"][rows, lanes(1)] * BF16(HD**-0.5), low_half)
        values = s["qkvv"][rows, lanes(2)]
        dctx = s["dctx"][rows, lanes(0)]
        dctx_heads = split_heads(dctx, low_half)
        cross = dctx.astype(F32) * s["ctx"][rows, lanes(0)].astype(F32)
        dscores = []
        for head in range(2):
            own = jnp.where(low_half == (head == 0), cross, 0.0)
            row_dot = jnp.sum(own, axis=-1, keepdims=True)
            dprobs = mm_bt(dctx_heads[head], values)
            probs = s["probs"][index * 2 + head].astype(F32)
            dscores.append((probs * (dprobs - row_dot)).astype(BF16))
        dquery = mm(jnp.concatenate(dscores, axis=1), jnp.concatenate(k_heads, axis=0))
        qt = jnp.concatenate([q_heads[0].T, q_heads[1].T], axis=1)
        dt = jnp.concatenate([dctx_heads[0].T, dctx_heads[1].T], axis=1)
        both = jnp.concatenate([s["probs"][index * 2], s["probs"][index * 2 + 1]], axis=0)
        dkey = mm(qt, jnp.concatenate(dscores, axis=0)).T
        dvalue = mm(dt, both).T
        s["dqkv"][rows, lanes(0)] = dquery.astype(BF16)
        s["dqkv"][rows, lanes(1)] = dkey.astype(BF16)
        s["dqkv"][rows, lanes(2)] = dvalue.astype(BF16)

    for index in range(PAIR * H // 2):
        attend(index)
    dqkv = s["dqkv"][...]
    s["gqkv"][...] += mm_at(s["n1"][...], dqkv)
    s["gbqkv"][...] += jnp.sum(dqkv.astype(F32), axis=0, keepdims=True)
    dnorm_a = mm_bt(dqkv, w["qkv"][...])
    put_mod(1, dnorm_a * normed_x)
    put_mod(0, dnorm_a)
    return grad_mid + norm_back(
        flat_rows(per_latent(dnorm_a) * (1.0 + scale_a)), normed_x, inv_a
    )


def pack_grads(order, chunk, me, activ, stage, flat, sem, w, s, out_grads, dactiv_ref):
    n, padded = stage.shape[0], stage.shape[1]

    def matrix(values_of, row, depth, width):
        count = width // LANES
        for c in range(count):
            flat[pl.ds(row + c, depth, stride=count), :] = values_of(c)

    def of_ref(ref):
        return lambda c: ref[:, c * LANES : (c + 1) * LANES]

    def vector(value, row, width, start=0):
        for c in range(width // LANES):
            flat[row + c : row + c + 1, :] = value[:, start + c * LANES : start + (c + 1) * LANES]

    dmods = jnp.concatenate([s["dmods"][latent] for latent in range(16)], axis=0).astype(BF16)
    dmods_wide = dmods.astype(F32)
    dactiv_ref[...] = mm_bt(dmods, w["ada"][...])
    left = activ[...]
    matrix(lambda c: mm_at(left, dmods[:, c * LANES : (c + 1) * LANES]), R_ADA, D, 6 * D)
    vector(jnp.sum(dmods_wide, axis=0, keepdims=True), R_BADA, 6 * D)
    matrix(of_ref(s["gqkv"]), R_QKV, D, 3 * D)
    vector(s["gbqkv"], R_BQ, D)
    vector(s["gbqkv"], R_BV, D, 2 * D)
    matrix(of_ref(s["go"]), R_O, D, D)
    vector(s["gbo"], R_BO, D)
    matrix(of_ref(s["g1"]), R_1, D, MLP)
    vector(s["gb1"], R_B1, MLP)
    matrix(lambda c: s["g2"][c * LANES : (c + 1) * LANES, :].T, R_2, MLP, D)
    vector(s["gb2"], R_B2, D)
    flat[R_END : flat.shape[0], :] = jnp.zeros((flat.shape[0] - R_END, LANES), F32)

    def gather(owner, carry):
        slot = slot_of(order[1], owner, me)
        stage[slot] = flat[pl.ds(owner * chunk, padded), :].astype(BF16)
        return carry

    lax.fori_loop(0, n, gather, 0)
    copy = pltpu.make_async_copy(stage, out_grads, sem.at[0])
    copy.start()
    copy.wait()


def backward_kernel(order, chunk, names, last, scalars, half_a, half_b, activ, x_ref, g_ref, *rest):
    if last:
        out_ref, *rest = rest
    gin_ref, dactiv_ref, out_grads, stage, flat, sem, *scratch = rest
    refs = dict(zip(names, scratch))
    step = pl.program_id(0)
    count, me = scalars[0], scalars[1]

    @pl.when(step == 0)
    def _():
        load_weights(order, chunk, me, half_a, half_b, activ, stage, flat, sem, refs)
        for name in ("gqkv", "go", "g1", "g2", "gbqkv", "gbo", "gb1", "gb2", "dmods"):
            refs[name][...] = jnp.zeros_like(refs[name])

    @pl.when(step * PAIR < count)
    def _():
        x = flat_rows(x_ref[...].astype(F32))
        result, branch, *kept = forward(step, x, refs, refs, True)
        grad = g_ref[...].astype(F32)
        if last:
            latent = lax.broadcasted_iota(jnp.int32, (PAIR, SEQ, D), 0) + step * PAIR
            live = latent < count
            out_ref[...] = jnp.where(live, per_latent(result), 0.0).astype(BF16)
            grad = jnp.where(live, grad, 0.0)
        gin_ref[...] = per_latent(
            backward_step(step, x, flat_rows(grad), refs, refs, branch, *kept)
        )

    @pl.when(step * PAIR >= count)
    def _():
        gin_ref[...] = jnp.zeros_like(gin_ref)
        if last:
            out_ref[...] = jnp.zeros_like(out_ref)

    @pl.when(step == pl.num_programs(0) - 1)
    def _():
        pack_grads(order, chunk, me, activ, stage, flat, sem, refs, refs, out_grads, dactiv_ref)


def scratch_of(parts):
    names, shapes = [], []
    for part in parts:
        for name, (shape, dtype) in part.items():
            names.append(name)
            shapes.append(pltpu.VMEM(shape, dtype))
    return tuple(names), shapes


def run_forward(order, chunk, scalars, halves, activ, x):
    n, padded = lax.axis_size("dev"), halves[0].shape[1]
    names, shapes = scratch_of([WEIGHT_SCRATCH, ACT_SCRATCH])
    block = pl.BlockSpec((PAIR, SEQ, D), lambda i, sc: (i, 0, 0))
    whole = pl.BlockSpec((16, D), lambda i, sc: (0, 0))
    hbm = pl.BlockSpec(memory_space=pl.ANY)
    return pl.pallas_call(
        functools.partial(forward_kernel, order, chunk, names),
        grid_spec=pltpu.PrefetchScalarGridSpec(
            num_scalar_prefetch=1,
            grid=(x.shape[0] // PAIR,),
            in_specs=[hbm, hbm, whole, block],
            out_specs=block,
            scratch_shapes=[
                pltpu.VMEM((n, padded, LANES), BF16),
                pltpu.VMEM(((n - 1) * chunk + padded, LANES), F32),
                pltpu.SemaphoreType.DMA((2,)),
            ]
            + shapes,
        ),
        out_shape=jax.ShapeDtypeStruct(x.shape, F32),
        compiler_params=pltpu.CompilerParams(vmem_limit_bytes=VMEM_LIMIT),
        cost_estimate=pl.CostEstimate(
            flops=8_000_000_000, bytes_accessed=20_000_000, transcendentals=6_000_000
        ),
        name="block_forward",
    )(scalars, *halves, activ, x)


def run_backward(order, chunk, scalars, halves, activ, x, grad, last):
    n, padded = lax.axis_size("dev"), halves[0].shape[1]
    names, shapes = scratch_of([WEIGHT_SCRATCH, ACT_SCRATCH, BACK_SCRATCH])
    block = pl.BlockSpec((PAIR, SEQ, D), lambda i, sc: (i, 0, 0))
    whole = pl.BlockSpec((16, D), lambda i, sc: (0, 0))
    hbm = pl.BlockSpec(memory_space=pl.ANY)
    outs = [
        jax.ShapeDtypeStruct(x.shape, F32),
        jax.ShapeDtypeStruct((16, D), F32),
        jax.ShapeDtypeStruct((n, padded, LANES), BF16),
    ]
    out_specs = [block, whole, hbm]
    if last:
        outs = [jax.ShapeDtypeStruct(x.shape, BF16)] + outs
        out_specs = [block] + out_specs
    return pl.pallas_call(
        functools.partial(backward_kernel, order, chunk, names, last),
        grid_spec=pltpu.PrefetchScalarGridSpec(
            num_scalar_prefetch=1,
            grid=(x.shape[0] // PAIR,),
            in_specs=[hbm, hbm, whole, block, block],
            out_specs=out_specs,
            scratch_shapes=[
                pltpu.VMEM((n, padded, LANES), BF16),
                pltpu.VMEM(((n - 1) * chunk + padded, LANES), F32),
                pltpu.SemaphoreType.DMA((2,)),
            ]
            + shapes,
        ),
        out_shape=outs,
        compiler_params=pltpu.CompilerParams(vmem_limit_bytes=VMEM_LIMIT),
        cost_estimate=pl.CostEstimate(
            flops=32_000_000_000, bytes_accessed=40_000_000, transcendentals=6_000_000
        ),
        name="block_backward",
    )(scalars, *halves, activ, x, grad)


def swap(values, bit, n):
    return lax.ppermute(values, "dev", [(i, i ^ (1 << bit)) for i in range(n)])


def add_low(kept, sent):
    return (kept.astype(F32) + sent.astype(F32)).astype(BF16)


def gather_halves(n, shard):
    bits = n.bit_length() - 1
    held = shard
    for bit in range(bits - 1, 2, -1):
        held = jnp.concatenate([held, swap(held, bit, n)], axis=0)
    rows = held.shape[1] // 2
    left, right = held[:, :rows], held[:, rows:]
    left = jnp.stack([left, swap(left, 2, n)], axis=0)
    right = jnp.stack([right, swap(right, 1, n)], axis=0)
    left = jnp.stack([left, swap(left, 1, n)], axis=0)
    right = jnp.stack([right, swap(right, 2, n)], axis=1)
    held = jnp.concatenate([left, right], axis=3).reshape((n // 2, 2 * rows, LANES))
    return held, swap(held, 0, n)


def halve(parts, bit, n):
    half = parts.shape[0] // 2
    return add_low(parts[:half], swap(parts[half:], bit, n))


def scatter_rest(order, n, parts, sent):
    parts = add_low(parts[: parts.shape[0] // 2], sent)
    for bit in order[-2::-1]:
        parts = halve(parts, bit, n)
    return parts.astype(F32)


def scatter_sum_split(n, parts):
    bits = n.bit_length() - 1
    parts = halve(parts, 0, n)
    rows = parts.shape[1] // 2
    parts = parts.reshape((2, 2, n // 8) + parts.shape[1:])
    left, right = parts[:, :, :, :rows], parts[:, :, :, rows:]
    left = add_low(left[0], swap(left[1], 1, n))
    right = add_low(right[:, 0], swap(right[:, 1], 2, n))
    left = add_low(left[0], swap(left[1], 2, n))
    right = add_low(right[0], swap(right[1], 1, n))
    parts = jnp.concatenate([left, right], axis=1)
    for bit in range(3, bits):
        parts = halve(parts, bit, n)
    return parts.astype(F32)


def shards(latents, cond, params, cotangent, counts):
    n = lax.axis_size("dev")
    chunk = params.shape[1] // LANES
    padded = (chunk + 31) // 32 * 32
    bits = n.bit_length() - 1
    first = tuple(range(bits - 1, -1, -1))
    second = first[:-3] + (2, 0, 1)
    scalars = jnp.stack([counts[0], lax.axis_index("dev").astype(jnp.int32)])
    cond_float = cond.astype(F32)
    activ = jax.nn.silu(cond_float).astype(BF16)
    activ = jnp.pad(activ, ((0, 16 - activ.shape[0]), (0, 0)))
    rows = params.reshape(LAYERS, chunk, LANES)
    rows = jnp.pad(rows, ((0, 0), (0, padded - chunk), (0, 0)))
    gathered = lax.all_gather(rows[1], "dev", axis=0)
    weights_2 = (gathered, gathered)
    weights_1 = gather_halves(n, rows[:1])
    middle = run_forward((first, first), chunk, scalars, weights_1, activ, latents)
    output, grad_mid, dactiv_2, parts_2 = run_backward(
        (None, second), chunk, scalars, weights_2, activ, middle, cotangent, True
    )
    sent_2 = swap(parts_2[n // 2 :], second[-1], n)
    grad_in, dactiv_1, parts_1 = run_backward(
        (first, first), chunk, scalars, weights_1, activ, latents, grad_mid, False
    )
    parts_1, sent_2 = lax.optimization_barrier((parts_1, sent_2))
    sum_2 = scatter_rest(second, n, parts_2, sent_2)
    sum_1 = scatter_sum_split(n, parts_1)
    param_grads = jnp.concatenate([sum_1, sum_2], axis=0)[:, :chunk].reshape(LAYERS, chunk * LANES)
    _, silu_pull = jax.vjp(jax.nn.silu, cond_float)
    cond_grad = silu_pull((dactiv_1 + dactiv_2)[: cond.shape[0]])[0]
    return (output, grad_in, cond_grad, param_grads)


def solution(mesh):
    return jax.shard_map(
        shards,
        mesh=mesh,
        in_specs=(
            P("dev", None, None),
            P("dev", None),
            P(None, "dev"),
            P("dev", None, None),
            P("dev"),
        ),
        out_specs=(P("dev", None, None), P("dev", None, None), P("dev", None), P(None, "dev")),
        check_vma=False,
    )
```
